128 devices in a mesh: gx: 4 (over x), gy: 8 (over y, core), gz: 4 (over z).
Axes of the slice: x: 4, y: 4, z: 4, core: 2. Of those that a mesh axis runs over, the one named last changes fastest.
Arguments:
- star_residual: bfloat16 [512, 64, 1152], P(('gx', 'gy', 'gz')), may hold values from -6 to 6
- patch_inverse: bfloat16 [512, 1152, 1152], P(('gx', 'gy', 'gz')), may hold values from -0.1875 to 0.1875
- block_owner: int32 [512, 9], P(('gx', 'gy', 'gz')), may hold values from 0 to 127, as said below
- block_slot: int32 [512, 9], P(('gx', 'gy', 'gz')), may hold values from 0 to 1, as said below
- recv_target: int32 [128, 27, 2], P(('gx', 'gy', 'gz')), may hold values from -1 to 7, as said below
Outputs:
- owned_sum: float32 [1024, 64, 128], P(('gx', 'gy', 'gz'))
- combined: float32 [512, 9, 64, 128], P(('gx', 'gy', 'gz'))
The draws below stay inside these ranges and needn't reach their ends.
Inputs may be any that keep to these rules, and one draw needn't show every extreme that they name: `block_owner`: each block's owner is the block's own partition or one whose coordinate differs by at most one step along each of the three mesh axes, counted with wrap-around. `block_slot`: blocks of one partition that have the same owner have distinct slots; in every partition some owner receives exactly 2 of its blocks. `recv_target`: every slot that a block uses maps to an owned block of its owner; slots that no block uses hold -1.
All inputs are finite; a program needn't handle non-finite values.
Results may differ from the reference program's by a relative error of at most 0.0003.
Values sent between devices are 32-bit elements; how exact they have to be, the bound alone decides.
No kernel may reach another device: no remote copies, remote signals or barrier semaphores. Data moves between devices by JAX's collectives and lax.ppermute only.
A program may use at most 64 MiB of HBM per device.

```python
import jax
import jax.numpy as jnp
from jax import lax

BW = 128
PDOF = 1152
PATCH_DEV = 4
RHS = 64
OWNB = 8
CAP = 2
NBLK = 9
PX = 4
PY = 8
PZ = 4
NDEV = 128
PATCHES = 512


def axis_deltas(extent):
    if extent == 1:
        return [0]
    if extent == 2:
        return [0, 1]
    return [-1, 0, 1]


def routing(key):
    offsets = [(a, b, c) for a in axis_deltas(PX) for b in axis_deltas(PY) for c in axis_deltas(PZ)]
    offset_total = len(offsets)
    step_x = jnp.array([o[0] for o in offsets], jnp.int32)
    step_y = jnp.array([o[1] for o in offsets], jnp.int32)
    step_z = jnp.array([o[2] for o in offsets], jnp.int32)
    codes = jnp.array([9 * (o[0] + 1) + 3 * (o[1] + 1) + (o[2] + 1) for o in offsets], jnp.int32)
    block_total = PATCH_DEV * NBLK
    base = jax.random.fold_in(key, 1301)

    def single(device):
        device_key = jax.random.fold_in(base, device)
        key_fav, key_score, key_assign = jax.random.split(device_key, 3)
        favored = jax.random.randint(key_fav, (), 0, offset_total)
        pairs = jnp.arange(offset_total * CAP, dtype=jnp.int32)
        scores = jax.random.permutation(key_score, offset_total * CAP).astype(jnp.int32)
        scores = jnp.where(pairs // CAP == favored, scores - offset_total * CAP, scores)
        ranked = jnp.argsort(scores, stable=True).astype(jnp.int32)
        chosen = ranked[:block_total]
        picked = chosen[jax.random.permutation(key_assign, block_total).astype(jnp.int32)]
        offset_ids = picked // CAP
        slot_ids = (picked % CAP).astype(jnp.int32)
        coord_x = device // (PY * PZ)
        coord_y = device // PZ % PY
        coord_z = device % PZ
        owner_ids = ((coord_x + step_x[offset_ids]) % PX * PY * PZ + (coord_y + step_y[offset_ids]) % PY * PZ + (coord_z + step_z[offset_ids]) % PZ).astype(jnp.int32)
        return (owner_ids, slot_ids, codes[offset_ids])
    owner_all, slot_all, code_all = jax.vmap(single)(jnp.arange(NDEV, dtype=jnp.int32))
    target_all = jax.random.randint(jax.random.fold_in(key, 2417), (NDEV, block_total), 0, OWNB).astype(jnp.int32)
    index_all = (owner_all * 27 * CAP + code_all * CAP + slot_all).reshape(-1)
    target_table = jnp.full((NDEV * 27 * CAP,), -1, jnp.int32).at[index_all].set(target_all.reshape(-1))
    return (owner_all.reshape(NDEV * PATCH_DEV, NBLK), slot_all.reshape(NDEV * PATCH_DEV, NBLK), target_table.reshape(NDEV, 27, CAP))


def draw_block_owner(key, part):
    return routing(key)[0]


def draw_block_slot(key, part):
    return routing(key)[1]


def draw_recv_target(key, part):
    return routing(key)[2]


def block_levels(key, shape, shards, least, top_value):
    loudness, own = 1.0, jax.random.fold_in(key, 6)
    for axis_at, shards_of in shards:
        heights = jnp.exp(jax.random.uniform(jax.random.fold_in(own, axis_at), (shards_of,), jnp.float32, least / len(shards), top_value / len(shards)))
        loudness = loudness * jnp.repeat(heights, shape[axis_at] // shards_of).reshape([-1 if axis == axis_at else 1 for axis in range(len(shape))])
    return loudness


def noise(own_key, dims, width, most, cuts=(), held_as=jnp.bfloat16):
    loudness = block_levels(own_key, dims, cuts, -0.22, 0.18) if cuts else 1.0
    values = jax.random.normal(own_key, dims, jnp.float32) * width * loudness
    return jnp.minimum(jnp.maximum(values, -most), most).astype(held_as)


def setup_inputs(seed: int = 0) -> dict:
    seeds = jax.random.split(jax.random.key(seed), 6)
    star_residual = noise(seeds[0], (PATCHES, RHS, PDOF), 1.0, 6.0, ((0, 128),))
    patch_inverse = noise(seeds[1], (PATCHES, PDOF, PDOF), PDOF ** -0.5, 0.1875, ((0, 128),))
    block_owner = draw_block_owner(jax.random.fold_in(seeds[5], 71), 0)
    block_slot = draw_block_slot(jax.random.fold_in(seeds[5], 71), 0)
    recv_target = draw_recv_target(jax.random.fold_in(seeds[5], 71), 0)
    return dict(star_residual=star_residual, patch_inverse=patch_inverse, block_owner=block_owner, block_slot=block_slot, recv_target=recv_target)


def axis_code(far_index, near_index, extent):
    distance = (far_index - near_index) % extent
    return jnp.where(distance == 0, 1, jnp.where(distance == 1, 2, 0)).astype(jnp.int32)


def offset_code(owner_ids, sender_ids):
    owner_x = owner_ids // (PY * PZ)
    owner_y = (owner_ids // PZ) % PY
    owner_z = owner_ids % PZ
    sender_x = sender_ids // (PY * PZ)
    sender_y = (sender_ids // PZ) % PY
    sender_z = sender_ids % PZ
    return (9 * axis_code(owner_x, sender_x, PX) + 3 * axis_code(owner_y, sender_y, PY)
            + axis_code(owner_z, sender_z, PZ)).astype(jnp.int32)


def reference(star_residual, patch_inverse, block_owner, block_slot, recv_target):
    residual_wide = star_residual.astype(jnp.float32)
    inverse_wide = patch_inverse.astype(jnp.float32).reshape(PATCHES, NBLK, BW, PDOF)
    contribution = jnp.einsum('prj,pbwj->pbrw', residual_wide, inverse_wide, precision=lax.Precision.HIGHEST)
    blocks = contribution.reshape(PATCHES * NBLK, RHS, BW)
    sender_ids = (jnp.arange(PATCHES * NBLK, dtype=jnp.int32) // (PATCH_DEV * NBLK)).astype(jnp.int32)
    owner_ids = block_owner.reshape(-1).astype(jnp.int32)
    slot_ids = block_slot.reshape(-1).astype(jnp.int32)
    codes = offset_code(owner_ids, sender_ids)
    targets = recv_target[owner_ids, codes, slot_ids].astype(jnp.int32)
    keys = (owner_ids * OWNB + targets).astype(jnp.int32)
    owned_sum = jax.ops.segment_sum(blocks, keys, num_segments=NDEV * OWNB)
    combined = owned_sum[keys].reshape(PATCHES, NBLK, RHS, BW)
    return owned_sum, combined
```

```python
import functools

import jax
import jax.numpy as jnp
from jax import lax
from jax.experimental import pallas as pl
from jax.experimental.pallas import tpu as pltpu
from jax.sharding import PartitionSpec as P

OWNB = 8
AXES = ("gx", "gy", "gz")
PLANE = [(dy, dz) for dy in (-1, 0, 1) for dz in (-1, 0, 1)]
HOME = PLANE.index((0, 0))
ABROAD = [i for i in range(len(PLANE)) if i != HOME]
VMEM = pltpu.VMEM
SMEM = pltpu.SMEM


def axis_code(far, near, extent):
    ahead = jnp.where(near == extent - 1, 0, near + 1)
    return jnp.where(far == near, 1, jnp.where(far == ahead, 2, 0))


def slot_index(owner, slot, extents, capacity):
    size_x, size_y, size_z = extents
    near = [lax.axis_index(a) for a in AXES]
    far_x = lax.div(owner, size_y * size_z)
    far_y = lax.rem(lax.div(owner, size_z), size_y)
    far_z = lax.rem(owner, size_z)
    code_x = axis_code(far_x, near[0], size_x)
    code_y = axis_code(far_y, near[1], size_y)
    code_z = axis_code(far_z, near[2], size_z)
    return ((code_y * 3 + code_z) * 3 + code_x) * capacity + slot


def contribute_kernel(extents, capacity, owner_ref, slot_ref, residual_ref, inverse_ref, *rest):
    outs, placed = rest[:-1], rest[-1]
    patch = pl.program_id(0)
    blocks = owner_ref.shape[1]
    width = inverse_ref.shape[1] // blocks
    product = lax.dot_general(
        residual_ref[0],
        inverse_ref[0],
        (((1,), (1,)), ((), ())),
        preferred_element_type=jnp.float32,
    )
    for b in range(blocks):
        at = slot_index(owner_ref[patch, b], slot_ref[patch, b], extents, capacity)
        placed[at] = product[:, b * width : (b + 1) * width]

    @pl.when(patch == pl.num_programs(0) - 1)
    def _():
        per = 3 * capacity
        for i, out in enumerate(outs):
            out[...] = placed[i * per : (i + 1) * per]


def contribute(owner, slot, residual, inverse, extents, capacity):
    patches, rhs, order = residual.shape
    width = order // owner.shape[1]
    per = 3 * capacity
    whole = pl.BlockSpec((per, rhs, width), lambda p: (0, 0, 0))
    return pl.pallas_call(
        functools.partial(contribute_kernel, extents, capacity),
        grid=(patches,),
        in_specs=[
            pl.BlockSpec(memory_space=SMEM),
            pl.BlockSpec(memory_space=SMEM),
            pl.BlockSpec((1, rhs, order), lambda p: (p, 0, 0)),
            pl.BlockSpec((1, order, order), lambda p: (p, 0, 0)),
        ],
        out_specs=[whole] * 9,
        out_shape=[jax.ShapeDtypeStruct((per, rhs, width), jnp.float32)] * 9,
        scratch_shapes=[VMEM((9 * per, rhs, width), jnp.float32)],
        compiler_params=pltpu.CompilerParams(vmem_limit_bytes=32 * 2**20),
    )(owner, slot, residual, inverse)


def table_entry(tables, cx, plane, c):
    dy, dz = PLANE[plane]
    return tables[cx][c, 9 * cx + 3 * (dy + 1) + (dz + 1)]


def gather_kernel(capacity, *refs):
    tables, arrived = refs[0:3], refs[3:12]
    outs, total = refs[12:15], refs[15]
    total[...] = jnp.zeros_like(total)
    for i in range(9):
        for cx in range(3):
            for c in range(capacity):
                t = table_entry(tables, cx, i, c)
                t = jnp.where(t < 0, OWNB, t)
                total[cx, t] += arrived[i][cx * capacity + c]
    for cx in range(3):
        outs[cx][...] = total[cx, :OWNB]


def gather(tables, arrived, capacity):
    _, rhs, width = arrived[0].shape
    return pl.pallas_call(
        functools.partial(gather_kernel, capacity),
        in_specs=[pl.BlockSpec(memory_space=SMEM)] * 3 + [pl.BlockSpec(memory_space=VMEM)] * 9,
        out_specs=[pl.BlockSpec(memory_space=VMEM)] * 3,
        out_shape=[jax.ShapeDtypeStruct((OWNB, rhs, width), jnp.float32)] * 3,
        scratch_shapes=[VMEM((3, OWNB + 1, rhs, width), jnp.float32)],
        compiler_params=pltpu.CompilerParams(vmem_limit_bytes=32 * 2**20),
    )(*tables, *arrived)


def answer_kernel(capacity, *refs):
    tables, totals, outs = refs[0:3], refs[3:6], refs[6:15]
    for i in range(9):
        for cx in range(3):
            for c in range(capacity):
                t = table_entry(tables, cx, i, c)
                outs[i][cx * capacity + c] = totals[cx][jnp.maximum(t, 0)]


def answer(tables, totals, capacity):
    _, rhs, width = totals[0].shape
    per = 3 * capacity
    return pl.pallas_call(
        functools.partial(answer_kernel, capacity),
        in_specs=[pl.BlockSpec(memory_space=SMEM)] * 3 + [pl.BlockSpec(memory_space=VMEM)] * 3,
        out_specs=[pl.BlockSpec(memory_space=VMEM)] * 9,
        out_shape=[jax.ShapeDtypeStruct((per, rhs, width), jnp.float32)] * 9,
        compiler_params=pltpu.CompilerParams(vmem_limit_bytes=32 * 2**20),
    )(*tables, *totals)


def collect_kernel(extents, capacity, owner_ref, slot_ref, *refs):
    returned, out, wide, back = refs[0:9], refs[9], refs[10], refs[11]
    patches, blocks = owner_ref.shape
    per = 3 * capacity
    for k in range(9 * per):
        back[k] = patches * blocks
    for p in range(patches):
        for b in range(blocks):
            at = slot_index(owner_ref[p, b], slot_ref[p, b], extents, capacity)
            back[at] = p * blocks + b
    for i in range(9):
        for k in range(per):
            wide[back[i * per + k]] = returned[i][k]
    for p in range(patches):
        out[p] = wide[p * blocks : (p + 1) * blocks]


def collect(owner, slot, returned, extents, capacity):
    patches, blocks = owner.shape
    _, rhs, width = returned[0].shape
    return pl.pallas_call(
        functools.partial(collect_kernel, extents, capacity),
        in_specs=[pl.BlockSpec(memory_space=SMEM)] * 2 + [pl.BlockSpec(memory_space=VMEM)] * 9,
        out_specs=pl.BlockSpec(memory_space=VMEM),
        out_shape=jax.ShapeDtypeStruct((patches, blocks, rhs, width), jnp.float32),
        scratch_shapes=[
            VMEM((patches * blocks + 1, rhs, width), jnp.float32),
            SMEM((27 * capacity,), jnp.int32),
        ],
        compiler_params=pltpu.CompilerParams(vmem_limit_bytes=32 * 2**20),
    )(owner, slot, *returned)


def shift(array, extents, by):
    size_x, size_y, size_z = extents
    pairs = []
    for x in range(size_x):
        for y in range(size_y):
            for z in range(size_z):
                to = ((x + by[0]) % size_x * size_y + (y + by[1]) % size_y) * size_z + (z + by[2]) % size_z
                pairs.append(((x * size_y + y) * size_z + z, to))
    return lax.ppermute(array, AXES, pairs)


def on_device(star_residual, patch_inverse, block_owner, block_slot, recv_target):
    extents = tuple(lax.axis_size(a) for a in AXES)
    capacity = recv_target.shape[2]
    table = jnp.swapaxes(recv_target, 1, 2)[0]
    tables = [shift(table, extents, (1, 0, 0)), table, shift(table, extents, (-1, 0, 0))]

    outgoing = contribute(block_owner, block_slot, star_residual, patch_inverse, extents, capacity)
    arrived = [
        outgoing[i] if i == HOME else shift(outgoing[i], extents, (0,) + PLANE[i]) for i in range(9)
    ]
    below, own, above = gather(tables, arrived, capacity)
    owned = own + shift(above, extents, (1, 0, 0)) + shift(below, extents, (-1, 0, 0))
    totals = [shift(owned, extents, (1, 0, 0)), owned, shift(owned, extents, (-1, 0, 0))]
    answers = answer(tables, totals, capacity)
    returned = [
        answers[i]
        if i == HOME
        else shift(answers[i], extents, (0, -PLANE[i][0], -PLANE[i][1]))
        for i in range(9)
    ]
    combined = collect(block_owner, block_slot, returned, extents, capacity)
    return owned, combined


def solution(mesh):
    return jax.shard_map(
        on_device,
        mesh=mesh,
        in_specs=(
            P(AXES, None, None),
            P(AXES, None, None),
            P(AXES, None),
            P(AXES, None),
            P(AXES, None, None),
        ),
        out_specs=(P(AXES, None, None), P(AXES, None, None, None)),
        check_vma=False,
    )
```

```python
import functools

import jax
import jax.numpy as jnp
from jax import lax
from jax.experimental import pallas as pl
from jax.experimental.pallas import tpu as pltpu
from jax.sharding import PartitionSpec as P

OWNB = 8
AXES = ("gx", "gy", "gz")
VMEM = pltpu.VMEM
SMEM = pltpu.SMEM

PLANE = [(1, 0), (-1, 0), (1, 2), (-1, 2), (0, 2), (1, 1), (-1, 1), (0, 1), (0, 0)]
HOME = len(PLANE) - 1


def toward(y, way):
    if way == 0:
        return y
    up = (y % 2 == 0) == (way == 1)
    return y + 1 if up else y - 1


def way_code(way, near_y):
    if way == 0:
        return 1
    even = lax.rem(near_y, 2) == 0
    return jnp.where(even, 2, 0) if way == 1 else jnp.where(even, 0, 2)


def axis_code(far, near, extent):
    ahead = jnp.where(near == extent - 1, 0, near + 1)
    return jnp.where(far == near, 1, jnp.where(far == ahead, 2, 0))


def place(owner, slot, near, extents, capacity):
    size_x, size_y, size_z = extents
    code_x = axis_code(lax.div(owner, size_y * size_z), near[0], size_x)
    code_y = axis_code(lax.rem(lax.div(owner, size_z), size_y), near[1], size_y)
    code_z = axis_code(lax.rem(owner, size_z), near[2], size_z)
    return ((code_x * 3 + code_y) * 3 + code_z) * capacity + slot


def contribute_kernel(extents, capacity, blocks, key_hbm, residual_hbm, inverse_hbm, *rest):
    outs = rest[:9]
    back, placed, key, residual, inverse, key_sem, res_sem, inv_sem = rest[9:]
    patches = inverse.shape[0]
    key_copy = pltpu.make_async_copy(key_hbm, key, key_sem)
    res_copy = pltpu.make_async_copy(residual_hbm, residual, res_sem)
    inv_copies = [
        pltpu.make_async_copy(inverse_hbm.at[p], inverse.at[p], inv_sem.at[p])
        for p in range(patches)
    ]
    key_copy.start()
    res_copy.start()
    for copy in inv_copies:
        copy.start()

    width = inverse.shape[1] // blocks
    near = [lax.axis_index(a) for a in AXES]
    per = 3 * capacity
    for k in range(9 * per):
        back[k] = patches * blocks
    key_copy.wait()
    at = []
    for p in range(patches):
        for b in range(blocks):
            owner, slot = lax.div(key[p, b], capacity), lax.rem(key[p, b], capacity)
            at.append(place(owner, slot, near, extents, capacity))
            back[at[-1]] = p * blocks + b
    res_copy.wait()
    for p in range(patches):
        inv_copies[p].wait()
        product = lax.dot_general(
            residual[p],
            inverse[p],
            (((1,), (1,)), ((), ())),
            preferred_element_type=jnp.float32,
        )
        for b in range(blocks):
            placed[at[p * blocks + b]] = product[:, b * width : (b + 1) * width]
    for i, (dx, way) in enumerate(PLANE):
        first = ((dx + 1) * 3 + way_code(way, near[1])) * per
        for k in range(per):
            outs[i][k] = placed[first + k]


def contribute(key, residual, inverse, extents, capacity):
    patches, rhs, order = residual.shape
    blocks = key.shape[1]
    width = order // blocks
    per = 3 * capacity
    return pl.pallas_call(
        functools.partial(contribute_kernel, extents, capacity, blocks),
        in_specs=[pl.BlockSpec(memory_space=pl.ANY)] * 3,
        out_specs=[pl.BlockSpec(memory_space=VMEM)] * 9 + [pl.BlockSpec(memory_space=SMEM)],
        out_shape=[jax.ShapeDtypeStruct((per, rhs, width), jnp.float32)] * 9
        + [jax.ShapeDtypeStruct((9 * per,), jnp.int32)],
        scratch_shapes=[
            VMEM((9 * per, rhs, width), jnp.float32),
            SMEM(key.shape, jnp.int32),
            VMEM(residual.shape, residual.dtype),
            VMEM(inverse.shape, inverse.dtype),
            pltpu.SemaphoreType.DMA,
            pltpu.SemaphoreType.DMA,
            pltpu.SemaphoreType.DMA((patches,)),
        ],
        compiler_params=pltpu.CompilerParams(vmem_limit_bytes=52 * 2**20),
    )(key, residual, inverse)


def entry(tables, plane, cz, c, near_y):
    dx, way = PLANE[plane]
    code_y = 1 if way == 0 else 2 - way_code(way, near_y)
    return tables[cz][c, 9 * (dx + 1) + 3 * code_y + cz]


def gather_kernel(capacity, *refs):
    tables, arrived = refs[0:3], refs[3:12]
    outs, total = refs[12:15], refs[15]
    near_y = lax.axis_index("gy")
    total[...] = jnp.zeros_like(total)
    for i in range(9):
        for cz in range(3):
            for c in range(capacity):
                t = entry(tables, i, cz, c, near_y)
                t = jnp.where(t < 0, OWNB, t)
                total[cz, t] += arrived[i][cz * capacity + c]
    for cz in range(3):
        outs[cz][...] = total[cz, :OWNB]


def gather(tables, arrived, capacity):
    _, rhs, width = arrived[0].shape
    return pl.pallas_call(
        functools.partial(gather_kernel, capacity),
        in_specs=[pl.BlockSpec(memory_space=SMEM)] * 3 + [pl.BlockSpec(memory_space=VMEM)] * 9,
        out_specs=[pl.BlockSpec(memory_space=VMEM)] * 3,
        out_shape=[jax.ShapeDtypeStruct((OWNB, rhs, width), jnp.float32)] * 3,
        scratch_shapes=[VMEM((3, OWNB + 1, rhs, width), jnp.float32)],
        compiler_params=pltpu.CompilerParams(vmem_limit_bytes=32 * 2**20),
    )(*tables, *arrived)


def answer_kernel(capacity, *refs):
    tables, totals, outs = refs[0:3], refs[3:6], refs[6:15]
    near_y = lax.axis_index("gy")
    for i in range(9):
        for cz in range(3):
            for c in range(capacity):
                t = entry(tables, i, cz, c, near_y)
                outs[i][cz * capacity + c] = totals[cz][jnp.maximum(t, 0)]


def answer(tables, totals, capacity):
    _, rhs, width = totals[0].shape
    per = 3 * capacity
    return pl.pallas_call(
        functools.partial(answer_kernel, capacity),
        in_specs=[pl.BlockSpec(memory_space=SMEM)] * 3 + [pl.BlockSpec(memory_space=VMEM)] * 3,
        out_specs=[pl.BlockSpec(memory_space=VMEM)] * 9,
        out_shape=[jax.ShapeDtypeStruct((per, rhs, width), jnp.float32)] * 9,
        compiler_params=pltpu.CompilerParams(vmem_limit_bytes=32 * 2**20),
    )(*tables, *totals)


def collect_kernel(capacity, patches, blocks, back, *refs):
    returned, out, wide = refs[0:9], refs[9], refs[10]
    near_y = lax.axis_index("gy")
    per = 3 * capacity
    for i, (dx, way) in enumerate(PLANE):
        first = ((dx + 1) * 3 + way_code(way, near_y)) * per
        for k in range(per):
            wide[back[first + k]] = returned[i][k]
    for p in range(patches):
        out[p] = wide[p * blocks : (p + 1) * blocks]


def collect(back, returned, patches, blocks, capacity):
    _, rhs, width = returned[0].shape
    return pl.pallas_call(
        functools.partial(collect_kernel, capacity, patches, blocks),
        in_specs=[pl.BlockSpec(memory_space=SMEM)] + [pl.BlockSpec(memory_space=VMEM)] * 9,
        out_specs=pl.BlockSpec(memory_space=VMEM),
        out_shape=jax.ShapeDtypeStruct((patches, blocks, rhs, width), jnp.float32),
        scratch_shapes=[VMEM((patches * blocks + 1, rhs, width), jnp.float32)],
        compiler_params=pltpu.CompilerParams(vmem_limit_bytes=32 * 2**20),
    )(back, *returned)


def move(array, extents, dx, way, dz):
    size_x, size_y, size_z = extents
    pairs = []
    for x in range(size_x):
        for y in range(size_y):
            for z in range(size_z):
                to_x, to_y, to_z = (x + dx) % size_x, toward(y, way) % size_y, (z + dz) % size_z
                pairs.append(
                    ((x * size_y + y) * size_z + z, (to_x * size_y + to_y) * size_z + to_z)
                )
    return lax.ppermute(array, AXES, pairs)


def on_device(star_residual, patch_inverse, block_owner, block_slot, recv_target):
    extents = tuple(lax.axis_size(a) for a in AXES)
    capacity = recv_target.shape[2]
    table = jnp.swapaxes(recv_target, 1, 2)[0]
    key = block_owner * capacity + block_slot
    *outgoing, back = contribute(key, star_residual, patch_inverse, extents, capacity)
    arrived = [
        outgoing[i] if i == HOME else move(outgoing[i], extents, dx, way, 0)
        for i, (dx, way) in enumerate(PLANE)
    ]
    table, arrived[7] = lax.optimization_barrier((table, arrived[7]))
    tables = [move(table, extents, 0, 0, 1), table, move(table, extents, 0, 0, -1)]
    below, own, above = gather(tables, arrived, capacity)
    owned = own + move(above, extents, 0, 0, 1) + move(below, extents, 0, 0, -1)
    totals = [move(owned, extents, 0, 0, 1), owned, move(owned, extents, 0, 0, -1)]
    answers = answer(tables, totals, capacity)
    returned = [
        answers[i] if i == HOME else move(answers[i], extents, -dx, way, 0)
        for i, (dx, way) in enumerate(PLANE)
    ]
    combined = collect(back, returned, *block_owner.shape, capacity)
    return owned, combined


def solution(mesh):
    return jax.shard_map(
        on_device,
        mesh=mesh,
        in_specs=(
            P(AXES, None, None),
            P(AXES, None, None),
            P(AXES, None),
            P(AXES, None),
            P(AXES, None, None),
        ),
        out_specs=(P(AXES, None, None), P(AXES, None, None, None)),
        check_vma=False,
    )
```

```python
import functools

import jax
import jax.numpy as jnp
from jax import lax
from jax.experimental import pallas as pl
from jax.experimental.pallas import tpu as pltpu
from jax.sharding import PartitionSpec as P

OWNB = 8
AXES = ("gx", "gy", "gz")
VMEM = pltpu.VMEM
SMEM = pltpu.SMEM

SIDE, LAST = 0, 2
PLANE = [(1, 0), (-1, 0), (1, 2), (-1, 2), (0, 2), (1, 1), (-1, 1), (0, 1), (0, 0)]
HOME = len(PLANE) - 1
OUT_ORDER = list(range(8))
BACK_ORDER = list(range(8))
TABLE_AFTER = 7
AHEAD = 2
FIRST = 2


def toward(y, way):
    if way == 0:
        return y
    up = (y % 2 == 0) == (way == 1)
    return y + 1 if up else y - 1


def way_code(way, near_y):
    if way == 0:
        return 1
    even = lax.rem(near_y, 2) == 0
    return jnp.where(even, 2, 0) if way == 1 else jnp.where(even, 0, 2)


def axis_code(far, near, extent):
    ahead = jnp.where(near == extent - 1, 0, near + 1)
    return jnp.where(far == near, 1, jnp.where(far == ahead, 2, 0))


def place(owner, slot, near, extents, capacity):
    size_x, size_y, size_z = extents
    code = [
        axis_code(lax.div(owner, size_y * size_z), near[0], size_x),
        axis_code(lax.rem(lax.div(owner, size_z), size_y), near[1], size_y),
        axis_code(lax.rem(owner, size_z), near[2], size_z),
    ]
    return ((code[SIDE] * 3 + code[1]) * 3 + code[LAST]) * capacity + slot


def contribute_kernel(extents, capacity, blocks, key_hbm, residual_hbm, inverse_hbm, *rest):
    outs = rest[:9]
    back, placed, key, residual, inverse, key_sem, res_sem, inv_sem = rest[9:]
    patches = inverse.shape[0]
    key_copy = pltpu.make_async_copy(key_hbm, key, key_sem)
    res_copy = pltpu.make_async_copy(residual_hbm, residual, res_sem)
    inv_copies = [
        pltpu.make_async_copy(inverse_hbm.at[p], inverse.at[p], inv_sem.at[p])
        for p in range(patches)
    ]
    key_copy.start()
    res_copy.start()
    for copy in inv_copies[:AHEAD]:
        copy.start()

    width = inverse.shape[1] // blocks
    near = [lax.axis_index(a) for a in AXES]
    per = 3 * capacity
    for k in range(9 * per):
        back[k] = patches * blocks
    key_copy.wait()
    at = []
    for p in range(patches):
        for b in range(blocks):
            owner, slot = lax.div(key[p, b], capacity), lax.rem(key[p, b], capacity)
            at.append(place(owner, slot, near, extents, capacity))
            back[at[-1]] = p * blocks + b
    res_copy.wait()
    for p in range(patches):
        inv_copies[p].wait()
        if p + AHEAD < patches:
            inv_copies[p + AHEAD].start()
        product = lax.dot_general(
            residual[p],
            inverse[p],
            (((1,), (1,)), ((), ())),
            preferred_element_type=jnp.float32,
        )
        for b in range(blocks):
            placed[at[p * blocks + b]] = product[:, b * width : (b + 1) * width]
    for i, (dx, way) in enumerate(PLANE):
        first = ((dx + 1) * 3 + way_code(way, near[1])) * per
        for k in range(per):
            outs[i][k] = placed[first + k]


def contribute(key, residual, inverse, extents, capacity):
    patches, rhs, order = residual.shape
    blocks = key.shape[1]
    width = order // blocks
    per = 3 * capacity
    return pl.pallas_call(
        functools.partial(contribute_kernel, extents, capacity, blocks),
        in_specs=[pl.BlockSpec(memory_space=pl.ANY)] * 3,
        out_specs=[pl.BlockSpec(memory_space=VMEM)] * 9 + [pl.BlockSpec(memory_space=SMEM)],
        out_shape=[jax.ShapeDtypeStruct((per, rhs, width), jnp.float32)] * 9
        + [jax.ShapeDtypeStruct((9 * per,), jnp.int32)],
        scratch_shapes=[
            VMEM((9 * per, rhs, width), jnp.float32),
            SMEM(key.shape, jnp.int32),
            VMEM(residual.shape, residual.dtype),
            VMEM(inverse.shape, inverse.dtype),
            pltpu.SemaphoreType.DMA,
            pltpu.SemaphoreType.DMA,
            pltpu.SemaphoreType.DMA((patches,)),
        ],
        compiler_params=pltpu.CompilerParams(vmem_limit_bytes=52 * 2**20),
    )(key, residual, inverse)


def entry(tables, plane, cz, c, near_y):
    dx, way = PLANE[plane]
    code_y = 1 if way == 0 else 2 - way_code(way, near_y)
    code = 9 * (dx + 1) + cz if SIDE == 0 else (dx + 1) + 9 * cz
    return tables[cz][c, code + 3 * code_y]


def gather_kernel(capacity, codes, *refs):
    count = len(codes)
    tables, arrived = dict(zip(codes, refs[:count])), refs[count : count + 9]
    outs, total = refs[count + 9 : -1], refs[-1]
    near_y = lax.axis_index("gy")
    total[...] = jnp.zeros_like(total)
    for i in range(9):
        for n, cz in enumerate(codes):
            for c in range(capacity):
                t = entry(tables, i, cz, c, near_y)
                t = jnp.where(t < 0, OWNB, t)
                total[n, t] += arrived[i][cz * capacity + c]
    for n in range(count):
        outs[n][...] = total[n, :OWNB]


def gather(tables, codes, arrived, capacity):
    _, rhs, width = arrived[0].shape
    return pl.pallas_call(
        functools.partial(gather_kernel, capacity, codes),
        in_specs=[pl.BlockSpec(memory_space=SMEM)] * len(codes)
        + [pl.BlockSpec(memory_space=VMEM)] * 9,
        out_specs=[pl.BlockSpec(memory_space=VMEM)] * len(codes),
        out_shape=[jax.ShapeDtypeStruct((OWNB, rhs, width), jnp.float32)] * len(codes),
        scratch_shapes=[VMEM((len(codes), OWNB + 1, rhs, width), jnp.float32)],
        compiler_params=pltpu.CompilerParams(vmem_limit_bytes=32 * 2**20),
    )(*[tables[cz] for cz in codes], *arrived)


def answer_kernel(capacity, steps, *refs):
    tables, totals, outs = refs[0:3], refs[3:6], refs[6:]
    near_y = lax.axis_index("gy")
    for out, i in zip(outs, steps):
        for cz in range(3):
            for c in range(capacity):
                t = entry(tables, i, cz, c, near_y)
                out[cz * capacity + c] = totals[cz][jnp.maximum(t, 0)]


def answer(tables, totals, steps, capacity):
    _, rhs, width = totals[0].shape
    per = 3 * capacity
    return pl.pallas_call(
        functools.partial(answer_kernel, capacity, steps),
        in_specs=[pl.BlockSpec(memory_space=SMEM)] * 3 + [pl.BlockSpec(memory_space=VMEM)] * 3,
        out_specs=[pl.BlockSpec(memory_space=VMEM)] * len(steps),
        out_shape=[jax.ShapeDtypeStruct((per, rhs, width), jnp.float32)] * len(steps),
        compiler_params=pltpu.CompilerParams(vmem_limit_bytes=32 * 2**20),
    )(*tables, *totals)


def collect_kernel(capacity, patches, blocks, back, *refs):
    returned, out, wide = refs[0:9], refs[9], refs[10]
    near_y = lax.axis_index("gy")
    per = 3 * capacity
    for i, (dx, way) in enumerate(PLANE):
        first = ((dx + 1) * 3 + way_code(way, near_y)) * per
        for k in range(per):
            wide[back[first + k]] = returned[i][k]
    for p in range(patches):
        out[p] = wide[p * blocks : (p + 1) * blocks]


def collect(back, returned, patches, blocks, capacity):
    _, rhs, width = returned[0].shape
    return pl.pallas_call(
        functools.partial(collect_kernel, capacity, patches, blocks),
        in_specs=[pl.BlockSpec(memory_space=SMEM)] + [pl.BlockSpec(memory_space=VMEM)] * 9,
        out_specs=pl.BlockSpec(memory_space=VMEM),
        out_shape=jax.ShapeDtypeStruct((patches, blocks, rhs, width), jnp.float32),
        scratch_shapes=[VMEM((patches * blocks + 1, rhs, width), jnp.float32)],
        compiler_params=pltpu.CompilerParams(vmem_limit_bytes=32 * 2**20),
    )(back, *returned)


def move(array, extents, side, way, last):
    by = [0, 0, 0]
    by[SIDE], by[LAST] = side, last
    size_x, size_y, size_z = extents
    pairs = []
    for x in range(size_x):
        for y in range(size_y):
            for z in range(size_z):
                to_x, to_y, to_z = (x + by[0]) % size_x, toward(y, way) % size_y, (z + by[2]) % size_z
                pairs.append(
                    ((x * size_y + y) * size_z + z, (to_x * size_y + to_y) * size_z + to_z)
                )
    return lax.ppermute(array, AXES, pairs)


def on_device(star_residual, patch_inverse, block_owner, block_slot, recv_target):
    extents = tuple(lax.axis_size(a) for a in AXES)
    capacity = recv_target.shape[2]
    table = jnp.swapaxes(recv_target, 1, 2)[0]
    key = block_owner * capacity + block_slot
    *outgoing, back = contribute(key, star_residual, patch_inverse, extents, capacity)
    arrived = [outgoing[HOME]] * 9
    for i in OUT_ORDER:
        arrived[i] = move(outgoing[i], extents, *PLANE[i], 0)
    table, arrived[TABLE_AFTER] = lax.optimization_barrier((table, arrived[TABLE_AFTER]))
    tables = [move(table, extents, 0, 0, 1), table, move(table, extents, 0, 0, -1)]
    below, above = gather(tables, (0, 2), arrived, capacity)
    (own,) = gather(tables, (1,), arrived, capacity)
    from_below = move(above, extents, 0, 0, 1)
    from_above = move(below, extents, 0, 0, -1)
    rising = own + from_below
    from_above, _ = lax.optimization_barrier((from_above, rising))
    sinking = own + from_above
    owned = rising + from_above
    total_below = move(rising, extents, 0, 0, 1) + below
    total_above = move(sinking, extents, 0, 0, -1) + above
    totals = [total_below, owned, total_above]
    answers = list(answer(tables, totals, tuple(range(FIRST)), capacity))
    answers += answer(tables, totals, tuple(range(FIRST, 9)), capacity)
    returned = [answers[HOME]] * 9
    for i in BACK_ORDER:
        returned[i] = move(answers[i], extents, -PLANE[i][0], PLANE[i][1], 0)
    combined = collect(back, returned, *block_owner.shape, capacity)
    return owned, combined


def solution(mesh):
    return jax.shard_map(
        on_device,
        mesh=mesh,
        in_specs=(
            P(AXES, None, None),
            P(AXES, None, None),
            P(AXES, None),
            P(AXES, None),
            P(AXES, None, None),
        ),
        out_specs=(P(AXES, None, None), P(AXES, None, None, None)),
        check_vma=False,
    )
```

```python
import functools

import jax
import jax.numpy as jnp
from jax import lax
from jax.experimental import pallas as pl
from jax.experimental.pallas import tpu as pltpu
from jax.sharding import PartitionSpec as P

OWNB = 8
AXES = ("gx", "gy", "gz")
VMEM = pltpu.VMEM
SMEM = pltpu.SMEM

SIDE, LAST = 0, 2
PLANE = [(1, 0), (-1, 0), (1, 2), (-1, 2), (0, 2), (1, 1), (-1, 1), (0, 1), (0, 0)]
HOME = len(PLANE) - 1
OUT_ORDER = list(range(8))
BACK_ORDER = list(range(8))
TABLE_AFTER = 7
EARLY = (8, 0, 1, 2)
AHEAD = 2
FIRST = 2


def toward(y, way):
    if way == 0:
        return y
    up = (y % 2 == 0) == (way == 1)
    return y + 1 if up else y - 1


def way_code(way, near_y):
    if way == 0:
        return 1
    even = lax.rem(near_y, 2) == 0
    return jnp.where(even, 2, 0) if way == 1 else jnp.where(even, 0, 2)


def axis_code(far, near, extent):
    ahead = jnp.where(near == extent - 1, 0, near + 1)
    return jnp.where(far == near, 1, jnp.where(far == ahead, 2, 0))


def place(owner, slot, near, extents, capacity):
    size_x, size_y, size_z = extents
    code = [
        axis_code(lax.div(owner, size_y * size_z), near[0], size_x),
        axis_code(lax.rem(lax.div(owner, size_z), size_y), near[1], size_y),
        axis_code(lax.rem(owner, size_z), near[2], size_z),
    ]
    return ((code[SIDE] * 3 + code[1]) * 3 + code[LAST]) * capacity + slot


def contribute_kernel(extents, capacity, blocks, key_hbm, residual_hbm, inverse_hbm, *rest):
    outs = rest[:9]
    placed, key, residual, inverse, key_sem, res_sem, inv_sem = rest[9:]
    patches = inverse.shape[0]
    key_copy = pltpu.make_async_copy(key_hbm, key, key_sem)
    res_copy = pltpu.make_async_copy(residual_hbm, residual, res_sem)
    inv_copies = [
        pltpu.make_async_copy(inverse_hbm.at[p], inverse.at[p], inv_sem.at[p])
        for p in range(patches)
    ]
    key_copy.start()
    res_copy.start()
    for copy in inv_copies[:AHEAD]:
        copy.start()

    width = inverse.shape[1] // blocks
    near = [lax.axis_index(a) for a in AXES]
    per = 3 * capacity
    key_copy.wait()
    at = []
    for p in range(patches):
        for b in range(blocks):
            owner, slot = lax.div(key[p, b], capacity), lax.rem(key[p, b], capacity)
            at.append(place(owner, slot, near, extents, capacity))
    res_copy.wait()
    for p in range(patches):
        inv_copies[p].wait()
        if p + AHEAD < patches:
            inv_copies[p + AHEAD].start()
        product = lax.dot_general(
            residual[p],
            inverse[p],
            (((1,), (1,)), ((), ())),
            preferred_element_type=jnp.float32,
        )
        for b in range(blocks):
            placed[at[p * blocks + b]] = product[:, b * width : (b + 1) * width]
    for i, (dx, way) in enumerate(PLANE):
        first = ((dx + 1) * 3 + way_code(way, near[1])) * per
        for k in range(per):
            outs[i][k] = placed[first + k]


def contribute(key, residual, inverse, extents, capacity):
    patches, rhs, order = residual.shape
    blocks = key.shape[1]
    width = order // blocks
    per = 3 * capacity
    return pl.pallas_call(
        functools.partial(contribute_kernel, extents, capacity, blocks),
        in_specs=[pl.BlockSpec(memory_space=pl.ANY)] * 3,
        out_specs=[pl.BlockSpec(memory_space=VMEM)] * 9,
        out_shape=[jax.ShapeDtypeStruct((per, rhs, width), jnp.float32)] * 9,
        scratch_shapes=[
            VMEM((9 * per, rhs, width), jnp.float32),
            SMEM(key.shape, jnp.int32),
            VMEM(residual.shape, residual.dtype),
            VMEM(inverse.shape, inverse.dtype),
            pltpu.SemaphoreType.DMA,
            pltpu.SemaphoreType.DMA,
            pltpu.SemaphoreType.DMA((patches,)),
        ],
        compiler_params=pltpu.CompilerParams(vmem_limit_bytes=52 * 2**20),
    )(key, residual, inverse)


def entry(tables, plane, cz, c, near_y):
    dx, way = PLANE[plane]
    code_y = 1 if way == 0 else 2 - way_code(way, near_y)
    code = 9 * (dx + 1) + cz if SIDE == 0 else (dx + 1) + 9 * cz
    return tables[cz][c, code + 3 * code_y]


def trace(back, key, extents, capacity):
    patches, blocks = key.shape
    near = [lax.axis_index(a) for a in AXES]
    for k in range(27 * capacity):
        back[k] = patches * blocks
    for p in range(patches):
        for b in range(blocks):
            owner, slot = lax.div(key[p, b], capacity), lax.rem(key[p, b], capacity)
            back[place(owner, slot, near, extents, capacity)] = p * blocks + b


def gather_own_kernel(capacity, extents, key, table, *refs):
    arrived, (out, back, total) = refs[:9], refs[9:]
    gather_kernel(capacity, (1,), table, *arrived, out, total)
    trace(back, key, extents, capacity)


def gather_own(key, table, arrived, extents, capacity):
    _, rhs, width = arrived[0].shape
    return pl.pallas_call(
        functools.partial(gather_own_kernel, capacity, extents),
        in_specs=[pl.BlockSpec(memory_space=SMEM)] * 2 + [pl.BlockSpec(memory_space=VMEM)] * 9,
        out_specs=[pl.BlockSpec(memory_space=VMEM), pl.BlockSpec(memory_space=SMEM)],
        out_shape=[
            jax.ShapeDtypeStruct((OWNB, rhs, width), jnp.float32),
            jax.ShapeDtypeStruct((27 * capacity,), jnp.int32),
        ],
        scratch_shapes=[VMEM((1, OWNB + 1, rhs, width), jnp.float32)],
        compiler_params=pltpu.CompilerParams(vmem_limit_bytes=32 * 2**20),
    )(key, table, *arrived)


def gather_kernel(capacity, codes, *refs):
    count = len(codes)
    tables, arrived = dict(zip(codes, refs[:count])), refs[count : count + 9]
    outs, total = refs[count + 9 : -1], refs[-1]
    near_y = lax.axis_index("gy")
    total[...] = jnp.zeros_like(total)
    for i in range(9):
        for n, cz in enumerate(codes):
            for c in range(capacity):
                t = entry(tables, i, cz, c, near_y)
                t = jnp.where(t < 0, OWNB, t)
                total[n, t] += arrived[i][cz * capacity + c]
    for n in range(count):
        outs[n][...] = total[n, :OWNB]


def gather(tables, codes, arrived, capacity):
    _, rhs, width = arrived[0].shape
    return pl.pallas_call(
        functools.partial(gather_kernel, capacity, codes),
        in_specs=[pl.BlockSpec(memory_space=SMEM)] * len(codes)
        + [pl.BlockSpec(memory_space=VMEM)] * 9,
        out_specs=[pl.BlockSpec(memory_space=VMEM)] * len(codes),
        out_shape=[jax.ShapeDtypeStruct((OWNB, rhs, width), jnp.float32)] * len(codes),
        scratch_shapes=[VMEM((len(codes), OWNB + 1, rhs, width), jnp.float32)],
        compiler_params=pltpu.CompilerParams(vmem_limit_bytes=32 * 2**20),
    )(*[tables[cz] for cz in codes], *arrived)


def answer_kernel(capacity, steps, *refs):
    tables, totals, outs = refs[0:3], refs[3:6], refs[6:]
    near_y = lax.axis_index("gy")
    for out, i in zip(outs, steps):
        for cz in range(3):
            for c in range(capacity):
                t = entry(tables, i, cz, c, near_y)
                out[cz * capacity + c] = totals[cz][jnp.maximum(t, 0)]


def answer(tables, totals, steps, capacity):
    _, rhs, width = totals[0].shape
    per = 3 * capacity
    return pl.pallas_call(
        functools.partial(answer_kernel, capacity, steps),
        in_specs=[pl.BlockSpec(memory_space=SMEM)] * 3 + [pl.BlockSpec(memory_space=VMEM)] * 3,
        out_specs=[pl.BlockSpec(memory_space=VMEM)] * len(steps),
        out_shape=[jax.ShapeDtypeStruct((per, rhs, width), jnp.float32)] * len(steps),
        compiler_params=pltpu.CompilerParams(vmem_limit_bytes=32 * 2**20),
    )(*tables, *totals)


def collect_kernel(capacity, blocks, steps, back, *refs):
    returned, (out, sems) = refs[: len(steps)], refs[-2:]
    near_y = lax.axis_index("gy")
    per = 3 * capacity
    jobs = []
    for i, step in enumerate(steps):
        dx, way = PLANE[step]
        first = ((dx + 1) * 3 + way_code(way, near_y)) * per
        for k in range(per):
            row = back[first + k]
            copy = pltpu.make_async_copy(returned[i].at[k], out.at[row], sems.at[i * per + k])
            jobs.append((row < blocks, copy))
    for used, copy in jobs:
        pl.when(used)(copy.start)
    for used, copy in jobs:
        pl.when(used)(copy.wait)


def collect(back, returned, steps, rows, capacity, out=None):
    _, rhs, width = returned[0].shape
    arrays = [back, *[returned[i] for i in steps]] + ([] if out is None else [out])
    return pl.pallas_call(
        functools.partial(collect_kernel, capacity, rows, steps),
        in_specs=[pl.BlockSpec(memory_space=SMEM)]
        + [pl.BlockSpec(memory_space=VMEM)] * len(steps)
        + [pl.BlockSpec(memory_space=pl.ANY)] * (out is not None),
        out_specs=pl.BlockSpec(memory_space=pl.ANY),
        out_shape=jax.ShapeDtypeStruct((rows, rhs, width), jnp.float32),
        scratch_shapes=[pltpu.SemaphoreType.DMA((len(steps) * 3 * capacity,))],
        input_output_aliases={} if out is None else {len(arrays) - 1: 0},
        compiler_params=pltpu.CompilerParams(vmem_limit_bytes=32 * 2**20),
    )(*arrays)


def move(array, extents, side, way, last):
    by = [0, 0, 0]
    by[SIDE], by[LAST] = side, last
    size_x, size_y, size_z = extents
    pairs = []
    for x in range(size_x):
        for y in range(size_y):
            for z in range(size_z):
                to_x, to_y, to_z = (x + by[0]) % size_x, toward(y, way) % size_y, (z + by[2]) % size_z
                pairs.append(
                    ((x * size_y + y) * size_z + z, (to_x * size_y + to_y) * size_z + to_z)
                )
    return lax.ppermute(array, AXES, pairs)


def on_device(star_residual, patch_inverse, block_owner, block_slot, recv_target):
    extents = tuple(lax.axis_size(a) for a in AXES)
    capacity = recv_target.shape[2]
    table = jnp.swapaxes(recv_target, 1, 2)[0]
    key = block_owner * capacity + block_slot
    outgoing = contribute(key, star_residual, patch_inverse, extents, capacity)
    arrived = [outgoing[HOME]] * 9
    for i in OUT_ORDER:
        arrived[i] = move(outgoing[i], extents, *PLANE[i], 0)
    table, arrived[TABLE_AFTER] = lax.optimization_barrier((table, arrived[TABLE_AFTER]))
    tables = [move(table, extents, 0, 0, 1), table, move(table, extents, 0, 0, -1)]
    below, above = gather(tables, (0, 2), arrived, capacity)
    own, back = gather_own(key, tables[1], arrived, extents, capacity)
    from_below = move(above, extents, 0, 0, 1)
    from_above = move(below, extents, 0, 0, -1)
    rising = own + from_below
    from_above, _ = lax.optimization_barrier((from_above, rising))
    sinking = own + from_above
    owned = rising + from_above
    total_below = move(rising, extents, 0, 0, 1) + below
    total_above = move(sinking, extents, 0, 0, -1) + above
    totals = [total_below, owned, total_above]
    answers = list(answer(tables, totals, tuple(range(FIRST)), capacity))
    answers += answer(tables, totals, tuple(range(FIRST, 9)), capacity)
    returned = [answers[HOME]] * 9
    for i in BACK_ORDER:
        returned[i] = move(answers[i], extents, -PLANE[i][0], PLANE[i][1], 0)
    patches, blocks = block_owner.shape
    rows = patches * blocks
    combined = collect(back, returned, EARLY, rows, capacity)
    late = tuple(i for i in range(9) if i not in EARLY)
    combined = collect(back, returned, late, rows, capacity, combined)
    combined = combined.reshape(patches, blocks, *combined.shape[1:])
    return owned, combined


def solution(mesh):
    return jax.shard_map(
        on_device,
        mesh=mesh,
        in_specs=(
            P(AXES, None, None),
            P(AXES, None, None),
            P(AXES, None),
            P(AXES, None),
            P(AXES, None, None),
        ),
        out_specs=(P(AXES, None, None), P(AXES, None, None, None)),
        check_vma=False,
    )
```

```python
import functools

import jax
import jax.numpy as jnp
from jax import lax
from jax.experimental import pallas as pl
from jax.experimental.pallas import tpu as pltpu
from jax.sharding import PartitionSpec as P

OWNB = 8
AXES = ("gx", "gy", "gz")
VMEM = pltpu.VMEM
SMEM = pltpu.SMEM

SIDE, LAST = 0, 2
PLANE = [(1, 0), (-1, 0), (1, 2), (-1, 2), (1, 1), (-1, 1), (0, 2), (0, 1), (0, 0)]
HOME = len(PLANE) - 1
OUT_ORDER = list(range(8))
BACK_ORDER = list(range(8))
TABLE_AFTER = 7
EARLY = (8, 0, 1, 2)
AHEAD = 2
FIRST = 2


def toward(y, way):
    if way == 0:
        return y
    up = (y % 2 == 0) == (way == 1)
    return y + 1 if up else y - 1


def way_code(way, near_y):
    if way == 0:
        return 1
    even = lax.rem(near_y, 2) == 0
    return jnp.where(even, 2, 0) if way == 1 else jnp.where(even, 0, 2)


def axis_code(far, near, extent):
    ahead = jnp.where(near == extent - 1, 0, near + 1)
    return jnp.where(far == near, 1, jnp.where(far == ahead, 2, 0))


def place(owner, slot, near, extents, capacity):
    size_x, size_y, size_z = extents
    code = [
        axis_code(lax.div(owner, size_y * size_z), near[0], size_x),
        axis_code(lax.rem(lax.div(owner, size_z), size_y), near[1], size_y),
        axis_code(lax.rem(owner, size_z), near[2], size_z),
    ]
    return ((code[SIDE] * 3 + code[1]) * 3 + code[LAST]) * capacity + slot


def contribute_kernel(extents, capacity, blocks, key_hbm, residual_hbm, inverse_hbm, *rest):
    outs = rest[:9]
    placed, key, residual, inverse, key_sem, res_sem, inv_sem = rest[9:]
    patches = inverse.shape[0]
    key_copy = pltpu.make_async_copy(key_hbm, key, key_sem)
    res_copy = pltpu.make_async_copy(residual_hbm, residual, res_sem)
    inv_copies = [
        pltpu.make_async_copy(inverse_hbm.at[p], inverse.at[p], inv_sem.at[p])
        for p in range(patches)
    ]
    key_copy.start()
    res_copy.start()
    for copy in inv_copies[:AHEAD]:
        copy.start()

    width = inverse.shape[1] // blocks
    near = [lax.axis_index(a) for a in AXES]
    per = 3 * capacity
    key_copy.wait()
    at = []
    for p in range(patches):
        for b in range(blocks):
            owner, slot = lax.div(key[p, b], capacity), lax.rem(key[p, b], capacity)
            at.append(place(owner, slot, near, extents, capacity))
    res_copy.wait()
    for p in range(patches):
        inv_copies[p].wait()
        if p + AHEAD < patches:
            inv_copies[p + AHEAD].start()
        product = lax.dot_general(
            residual[p],
            inverse[p],
            (((1,), (1,)), ((), ())),
            preferred_element_type=jnp.float32,
        )
        for b in range(blocks):
            placed[at[p * blocks + b]] = product[:, b * width : (b + 1) * width]
    for i, (dx, way) in enumerate(PLANE):
        first = ((dx + 1) * 3 + way_code(way, near[1])) * per
        for k in range(per):
            outs[i][k] = placed[first + k]


def contribute(key, residual, inverse, extents, capacity):
    patches, rhs, order = residual.shape
    blocks = key.shape[1]
    width = order // blocks
    per = 3 * capacity
    return pl.pallas_call(
        functools.partial(contribute_kernel, extents, capacity, blocks),
        in_specs=[pl.BlockSpec(memory_space=pl.ANY)] * 3,
        out_specs=[pl.BlockSpec(memory_space=VMEM)] * 9,
        out_shape=[jax.ShapeDtypeStruct((per, rhs, width), jnp.float32)] * 9,
        scratch_shapes=[
            VMEM((9 * per, rhs, width), jnp.float32),
            SMEM(key.shape, jnp.int32),
            VMEM(residual.shape, residual.dtype),
            VMEM(inverse.shape, inverse.dtype),
            pltpu.SemaphoreType.DMA,
            pltpu.SemaphoreType.DMA,
            pltpu.SemaphoreType.DMA((patches,)),
        ],
        compiler_params=pltpu.CompilerParams(vmem_limit_bytes=52 * 2**20),
    )(key, residual, inverse)


def entry(tables, plane, cz, c, near_y):
    dx, way = PLANE[plane]
    code_y = 1 if way == 0 else 2 - way_code(way, near_y)
    code = 9 * (dx + 1) + cz if SIDE == 0 else (dx + 1) + 9 * cz
    return tables[cz][c, code + 3 * code_y]


def trace(back, key, extents, capacity):
    patches, blocks = key.shape
    near = [lax.axis_index(a) for a in AXES]
    for k in range(27 * capacity):
        back[k] = patches * blocks
    for p in range(patches):
        for b in range(blocks):
            owner, slot = lax.div(key[p, b], capacity), lax.rem(key[p, b], capacity)
            back[place(owner, slot, near, extents, capacity)] = p * blocks + b


def gather_own_kernel(capacity, extents, key, table, *refs):
    arrived, (out, back, total) = refs[:9], refs[9:]
    gather_kernel(capacity, (1,), table, *arrived, out, total)
    trace(back, key, extents, capacity)


def gather_own(key, table, arrived, extents, capacity):
    _, rhs, width = arrived[0].shape
    return pl.pallas_call(
        functools.partial(gather_own_kernel, capacity, extents),
        in_specs=[pl.BlockSpec(memory_space=SMEM)] * 2 + [pl.BlockSpec(memory_space=VMEM)] * 9,
        out_specs=[pl.BlockSpec(memory_space=VMEM), pl.BlockSpec(memory_space=SMEM)],
        out_shape=[
            jax.ShapeDtypeStruct((OWNB, rhs, width), jnp.float32),
            jax.ShapeDtypeStruct((27 * capacity,), jnp.int32),
        ],
        scratch_shapes=[VMEM((1, OWNB + 1, rhs, width), jnp.float32)],
        compiler_params=pltpu.CompilerParams(vmem_limit_bytes=32 * 2**20),
    )(key, table, *arrived)


def gather_kernel(capacity, codes, *refs):
    count = len(codes)
    tables, arrived = dict(zip(codes, refs[:count])), refs[count : count + 9]
    outs, total = refs[count + 9 : -1], refs[-1]
    near_y = lax.axis_index("gy")
    total[...] = jnp.zeros_like(total)
    for i in range(9):
        for n, cz in enumerate(codes):
            for c in range(capacity):
                t = entry(tables, i, cz, c, near_y)
                t = jnp.where(t < 0, OWNB, t)
                total[n, t] += arrived[i][cz * capacity + c]
    for n in range(count):
        outs[n][...] = total[n, :OWNB]


def gather(tables, codes, arrived, capacity):
    _, rhs, width = arrived[0].shape
    return pl.pallas_call(
        functools.partial(gather_kernel, capacity, codes),
        in_specs=[pl.BlockSpec(memory_space=SMEM)] * len(codes)
        + [pl.BlockSpec(memory_space=VMEM)] * 9,
        out_specs=[pl.BlockSpec(memory_space=VMEM)] * len(codes),
        out_shape=[jax.ShapeDtypeStruct((OWNB, rhs, width), jnp.float32)] * len(codes),
        scratch_shapes=[VMEM((len(codes), OWNB + 1, rhs, width), jnp.float32)],
        compiler_params=pltpu.CompilerParams(vmem_limit_bytes=32 * 2**20),
    )(*[tables[cz] for cz in codes], *arrived)


def answer_kernel(capacity, steps, *refs):
    tables, totals, outs = refs[0:3], refs[3:6], refs[6:]
    near_y = lax.axis_index("gy")
    for out, i in zip(outs, steps):
        for cz in range(3):
            for c in range(capacity):
                t = entry(tables, i, cz, c, near_y)
                out[cz * capacity + c] = totals[cz][jnp.maximum(t, 0)]


def answer(tables, totals, steps, capacity):
    _, rhs, width = totals[0].shape
    per = 3 * capacity
    return pl.pallas_call(
        functools.partial(answer_kernel, capacity, steps),
        in_specs=[pl.BlockSpec(memory_space=SMEM)] * 3 + [pl.BlockSpec(memory_space=VMEM)] * 3,
        out_specs=[pl.BlockSpec(memory_space=VMEM)] * len(steps),
        out_shape=[jax.ShapeDtypeStruct((per, rhs, width), jnp.float32)] * len(steps),
        compiler_params=pltpu.CompilerParams(vmem_limit_bytes=32 * 2**20),
    )(*tables, *totals)


def collect_kernel(capacity, blocks, steps, back, *refs):
    returned, (out, sems) = refs[: len(steps)], refs[-2:]
    near_y = lax.axis_index("gy")
    per = 3 * capacity
    jobs = []
    for i, step in enumerate(steps):
        dx, way = PLANE[step]
        first = ((dx + 1) * 3 + way_code(way, near_y)) * per
        for k in range(per):
            row = back[first + k]
            copy = pltpu.make_async_copy(returned[i].at[k], out.at[row], sems.at[i * per + k])
            jobs.append((row < blocks, copy))
    for used, copy in jobs:
        pl.when(used)(copy.start)
    for used, copy in jobs:
        pl.when(used)(copy.wait)


def collect(back, returned, steps, rows, capacity, out=None):
    _, rhs, width = returned[0].shape
    arrays = [back, *[returned[i] for i in steps]] + ([] if out is None else [out])
    return pl.pallas_call(
        functools.partial(collect_kernel, capacity, rows, steps),
        in_specs=[pl.BlockSpec(memory_space=SMEM)]
        + [pl.BlockSpec(memory_space=VMEM)] * len(steps)
        + [pl.BlockSpec(memory_space=pl.ANY)] * (out is not None),
        out_specs=pl.BlockSpec(memory_space=pl.ANY),
        out_shape=jax.ShapeDtypeStruct((rows, rhs, width), jnp.float32),
        scratch_shapes=[pltpu.SemaphoreType.DMA((len(steps) * 3 * capacity,))],
        input_output_aliases={} if out is None else {len(arrays) - 1: 0},
        compiler_params=pltpu.CompilerParams(vmem_limit_bytes=32 * 2**20),
    )(*arrays)


def move(array, extents, side, way, last):
    by = [0, 0, 0]
    by[SIDE], by[LAST] = side, last
    size_x, size_y, size_z = extents
    pairs = []
    for x in range(size_x):
        for y in range(size_y):
            for z in range(size_z):
                to_x, to_y, to_z = (x + by[0]) % size_x, toward(y, way) % size_y, (z + by[2]) % size_z
                pairs.append(
                    ((x * size_y + y) * size_z + z, (to_x * size_y + to_y) * size_z + to_z)
                )
    return lax.ppermute(array, AXES, pairs)


def on_device(star_residual, patch_inverse, block_owner, block_slot, recv_target):
    extents = tuple(lax.axis_size(a) for a in AXES)
    capacity = recv_target.shape[2]
    table = jnp.swapaxes(recv_target, 1, 2)[0]
    key = block_owner * capacity + block_slot
    outgoing = contribute(key, star_residual, patch_inverse, extents, capacity)
    arrived = [outgoing[HOME]] * 9
    for i in OUT_ORDER:
        arrived[i] = move(outgoing[i], extents, *PLANE[i], 0)
    table, arrived[TABLE_AFTER] = lax.optimization_barrier((table, arrived[TABLE_AFTER]))
    tables = [move(table, extents, 0, 0, 1), table, move(table, extents, 0, 0, -1)]
    below, above = gather(tables, (0, 2), arrived, capacity)
    own, back = gather_own(key, tables[1], arrived, extents, capacity)
    from_below = move(above, extents, 0, 0, 1)
    from_above = move(below, extents, 0, 0, -1)
    rising = own + from_below
    from_above, _ = lax.optimization_barrier((from_above, rising))
    sinking = own + from_above
    owned = rising + from_above
    total_below = move(rising, extents, 0, 0, 1) + below
    total_above = move(sinking, extents, 0, 0, -1) + above
    totals = [total_below, owned, total_above]
    answers = list(answer(tables, totals, tuple(range(FIRST)), capacity))
    answers += answer(tables, totals, tuple(range(FIRST, 9)), capacity)
    returned = [answers[HOME]] * 9
    for i in BACK_ORDER:
        returned[i] = move(answers[i], extents, -PLANE[i][0], PLANE[i][1], 0)
    patches, blocks = block_owner.shape
    rows = patches * blocks
    combined = collect(back, returned, EARLY, rows, capacity)
    late = tuple(i for i in range(9) if i not in EARLY)
    combined = collect(back, returned, late, rows, capacity, combined)
    combined = combined.reshape(patches, blocks, *combined.shape[1:])
    return owned, combined


def solution(mesh):
    return jax.shard_map(
        on_device,
        mesh=mesh,
        in_specs=(
            P(AXES, None, None),
            P(AXES, None, None),
            P(AXES, None),
            P(AXES, None),
            P(AXES, None, None),
        ),
        out_specs=(P(AXES, None, None), P(AXES, None, None, None)),
        check_vma=False,
    )
```

```python
import functools

import jax
import jax.numpy as jnp
from jax import lax
from jax.experimental import pallas as pl
from jax.experimental.pallas import tpu as pltpu
from jax.sharding import PartitionSpec as P

OWNB = 8
AXES = ("gx", "gy", "gz")
VMEM = pltpu.VMEM
SMEM = pltpu.SMEM

SIDE, LAST = 0, 2
PLANE = [(1, 0), (-1, 0), (1, 2), (-1, 2), (-1, 1), (1, 1), (0, 2), (0, 1), (0, 0)]
HOME = len(PLANE) - 1
OUT_ORDER = list(range(8))
BACK_ORDER = list(range(8))
TABLE_AFTER = 7
EARLY = (8, 0, 1, 2)
AHEAD = 2
FIRST = 2


def toward(y, way):
    if way == 0:
        return y
    up = (y % 2 == 0) == (way == 1)
    return y + 1 if up else y - 1


def way_code(way, near_y):
    if way == 0:
        return 1
    even = lax.rem(near_y, 2) == 0
    return jnp.where(even, 2, 0) if way == 1 else jnp.where(even, 0, 2)


def axis_code(far, near, extent):
    ahead = jnp.where(near == extent - 1, 0, near + 1)
    return jnp.where(far == near, 1, jnp.where(far == ahead, 2, 0))


def place(owner, slot, near, extents, capacity):
    size_x, size_y, size_z = extents
    code = [
        axis_code(lax.div(owner, size_y * size_z), near[0], size_x),
        axis_code(lax.rem(lax.div(owner, size_z), size_y), near[1], size_y),
        axis_code(lax.rem(owner, size_z), near[2], size_z),
    ]
    return ((code[SIDE] * 3 + code[1]) * 3 + code[LAST]) * capacity + slot


def contribute_kernel(extents, capacity, blocks, key_hbm, residual_hbm, inverse_hbm, *rest):
    outs = rest[:9]
    placed, key, residual, inverse, key_sem, res_sem, inv_sem = rest[9:]
    patches = inverse.shape[0]
    key_copy = pltpu.make_async_copy(key_hbm, key, key_sem)
    res_copy = pltpu.make_async_copy(residual_hbm, residual, res_sem)
    inv_copies = [
        pltpu.make_async_copy(inverse_hbm.at[p], inverse.at[p], inv_sem.at[p])
        for p in range(patches)
    ]
    key_copy.start()
    res_copy.start()
    for copy in inv_copies[:AHEAD]:
        copy.start()

    width = inverse.shape[1] // blocks
    near = [lax.axis_index(a) for a in AXES]
    per = 3 * capacity
    key_copy.wait()
    at = []
    for p in range(patches):
        for b in range(blocks):
            owner, slot = lax.div(key[p, b], capacity), lax.rem(key[p, b], capacity)
            at.append(place(owner, slot, near, extents, capacity))
    res_copy.wait()
    for p in range(patches):
        inv_copies[p].wait()
        if p + AHEAD < patches:
            inv_copies[p + AHEAD].start()
        product = lax.dot_general(
            residual[p],
            inverse[p],
            (((1,), (1,)), ((), ())),
            preferred_element_type=jnp.float32,
        )
        for b in range(blocks):
            placed[at[p * blocks + b]] = product[:, b * width : (b + 1) * width]
    for i, (dx, way) in enumerate(PLANE):
        first = ((dx + 1) * 3 + way_code(way, near[1])) * per
        for k in range(per):
            outs[i][k] = placed[first + k]


def contribute(key, residual, inverse, extents, capacity):
    patches, rhs, order = residual.shape
    blocks = key.shape[1]
    width = order // blocks
    per = 3 * capacity
    return pl.pallas_call(
        functools.partial(contribute_kernel, extents, capacity, blocks),
        in_specs=[pl.BlockSpec(memory_space=pl.ANY)] * 3,
        out_specs=[pl.BlockSpec(memory_space=VMEM)] * 9,
        out_shape=[jax.ShapeDtypeStruct((per, rhs, width), jnp.float32)] * 9,
        scratch_shapes=[
            VMEM((9 * per, rhs, width), jnp.float32),
            SMEM(key.shape, jnp.int32),
            VMEM(residual.shape, residual.dtype),
            VMEM(inverse.shape, inverse.dtype),
            pltpu.SemaphoreType.DMA,
            pltpu.SemaphoreType.DMA,
            pltpu.SemaphoreType.DMA((patches,)),
        ],
        compiler_params=pltpu.CompilerParams(vmem_limit_bytes=52 * 2**20),
    )(key, residual, inverse)


def entry(tables, plane, cz, c, near_y):
    dx, way = PLANE[plane]
    code_y = 1 if way == 0 else 2 - way_code(way, near_y)
    code = 9 * (dx + 1) + cz if SIDE == 0 else (dx + 1) + 9 * cz
    return tables[cz][c, code + 3 * code_y]


def trace(back, key, extents, capacity):
    patches, blocks = key.shape
    near = [lax.axis_index(a) for a in AXES]
    for k in range(27 * capacity):
        back[k] = patches * blocks
    for p in range(patches):
        for b in range(blocks):
            owner, slot = lax.div(key[p, b], capacity), lax.rem(key[p, b], capacity)
            back[place(owner, slot, near, extents, capacity)] = p * blocks + b


def gather_own_kernel(capacity, extents, key, table, *refs):
    arrived, (out, back, total) = refs[:9], refs[9:]
    gather_kernel(capacity, (1,), table, *arrived, out, total)
    trace(back, key, extents, capacity)


def gather_own(key, table, arrived, extents, capacity):
    _, rhs, width = arrived[0].shape
    return pl.pallas_call(
        functools.partial(gather_own_kernel, capacity, extents),
        in_specs=[pl.BlockSpec(memory_space=SMEM)] * 2 + [pl.BlockSpec(memory_space=VMEM)] * 9,
        out_specs=[pl.BlockSpec(memory_space=VMEM), pl.BlockSpec(memory_space=SMEM)],
        out_shape=[
            jax.ShapeDtypeStruct((OWNB, rhs, width), jnp.float32),
            jax.ShapeDtypeStruct((27 * capacity,), jnp.int32),
        ],
        scratch_shapes=[VMEM((1, OWNB + 1, rhs, width), jnp.float32)],
        compiler_params=pltpu.CompilerParams(vmem_limit_bytes=32 * 2**20),
    )(key, table, *arrived)


def gather_kernel(capacity, codes, *refs):
    count = len(codes)
    tables, arrived = dict(zip(codes, refs[:count])), refs[count : count + 9]
    outs, total = refs[count + 9 : -1], refs[-1]
    near_y = lax.axis_index("gy")
    total[...] = jnp.zeros_like(total)
    for i in range(9):
        for n, cz in enumerate(codes):
            for c in range(capacity):
                t = entry(tables, i, cz, c, near_y)
                t = jnp.where(t < 0, OWNB, t)
                total[n, t] += arrived[i][cz * capacity + c]
    for n in range(count):
        outs[n][...] = total[n, :OWNB]


def gather(tables, codes, arrived, capacity):
    _, rhs, width = arrived[0].shape
    return pl.pallas_call(
        functools.partial(gather_kernel, capacity, codes),
        in_specs=[pl.BlockSpec(memory_space=SMEM)] * len(codes)
        + [pl.BlockSpec(memory_space=VMEM)] * 9,
        out_specs=[pl.BlockSpec(memory_space=VMEM)] * len(codes),
        out_shape=[jax.ShapeDtypeStruct((OWNB, rhs, width), jnp.float32)] * len(codes),
        scratch_shapes=[VMEM((len(codes), OWNB + 1, rhs, width), jnp.float32)],
        compiler_params=pltpu.CompilerParams(vmem_limit_bytes=32 * 2**20),
    )(*[tables[cz] for cz in codes], *arrived)


def answer_kernel(capacity, steps, *refs):
    tables, totals, outs = refs[0:3], refs[3:6], refs[6:]
    near_y = lax.axis_index("gy")
    for out, i in zip(outs, steps):
        for cz in range(3):
            for c in range(capacity):
                t = entry(tables, i, cz, c, near_y)
                out[cz * capacity + c] = totals[cz][jnp.maximum(t, 0)]


def answer(tables, totals, steps, capacity):
    _, rhs, width = totals[0].shape
    per = 3 * capacity
    return pl.pallas_call(
        functools.partial(answer_kernel, capacity, steps),
        in_specs=[pl.BlockSpec(memory_space=SMEM)] * 3 + [pl.BlockSpec(memory_space=VMEM)] * 3,
        out_specs=[pl.BlockSpec(memory_space=VMEM)] * len(steps),
        out_shape=[jax.ShapeDtypeStruct((per, rhs, width), jnp.float32)] * len(steps),
        compiler_params=pltpu.CompilerParams(vmem_limit_bytes=32 * 2**20),
    )(*tables, *totals)


def collect_kernel(capacity, blocks, steps, back, *refs):
    returned, (out, sems) = refs[: len(steps)], refs[-2:]
    near_y = lax.axis_index("gy")
    per = 3 * capacity
    jobs = []
    for i, step in enumerate(steps):
        dx, way = PLANE[step]
        first = ((dx + 1) * 3 + way_code(way, near_y)) * per
        for k in range(per):
            row = back[first + k]
            copy = pltpu.make_async_copy(returned[i].at[k], out.at[row], sems.at[i * per + k])
            jobs.append((row < blocks, copy))
    for used, copy in jobs:
        pl.when(used)(copy.start)
    for used, copy in jobs:
        pl.when(used)(copy.wait)


def collect(back, returned, steps, rows, capacity, out=None):
    _, rhs, width = returned[0].shape
    arrays = [back, *[returned[i] for i in steps]] + ([] if out is None else [out])
    return pl.pallas_call(
        functools.partial(collect_kernel, capacity, rows, steps),
        in_specs=[pl.BlockSpec(memory_space=SMEM)]
        + [pl.BlockSpec(memory_space=VMEM)] * len(steps)
        + [pl.BlockSpec(memory_space=pl.ANY)] * (out is not None),
        out_specs=pl.BlockSpec(memory_space=pl.ANY),
        out_shape=jax.ShapeDtypeStruct((rows, rhs, width), jnp.float32),
        scratch_shapes=[pltpu.SemaphoreType.DMA((len(steps) * 3 * capacity,))],
        input_output_aliases={} if out is None else {len(arrays) - 1: 0},
        compiler_params=pltpu.CompilerParams(vmem_limit_bytes=32 * 2**20),
    )(*arrays)


def move(array, extents, side, way, last):
    by = [0, 0, 0]
    by[SIDE], by[LAST] = side, last
    size_x, size_y, size_z = extents
    pairs = []
    for x in range(size_x):
        for y in range(size_y):
            for z in range(size_z):
                to_x, to_y, to_z = (x + by[0]) % size_x, toward(y, way) % size_y, (z + by[2]) % size_z
                pairs.append(
                    ((x * size_y + y) * size_z + z, (to_x * size_y + to_y) * size_z + to_z)
                )
    return lax.ppermute(array, AXES, pairs)


def on_device(star_residual, patch_inverse, block_owner, block_slot, recv_target):
    extents = tuple(lax.axis_size(a) for a in AXES)
    capacity = recv_target.shape[2]
    table = jnp.swapaxes(recv_target, 1, 2)[0]
    key = block_owner * capacity + block_slot
    outgoing = contribute(key, star_residual, patch_inverse, extents, capacity)
    arrived = [outgoing[HOME]] * 9
    for i in OUT_ORDER:
        arrived[i] = move(outgoing[i], extents, *PLANE[i], 0)
    table, arrived[TABLE_AFTER] = lax.optimization_barrier((table, arrived[TABLE_AFTER]))
    tables = [move(table, extents, 0, 0, 1), table, move(table, extents, 0, 0, -1)]
    below, above = gather(tables, (0, 2), arrived, capacity)
    own, back = gather_own(key, tables[1], arrived, extents, capacity)
    from_below = move(above, extents, 0, 0, 1)
    from_above = move(below, extents, 0, 0, -1)
    rising = own + from_below
    from_above, _ = lax.optimization_barrier((from_above, rising))
    sinking = own + from_above
    owned = rising + from_above
    total_below = move(rising, extents, 0, 0, 1) + below
    total_above = move(sinking, extents, 0, 0, -1) + above
    totals = [total_below, owned, total_above]
    answers = list(answer(tables, totals, tuple(range(FIRST)), capacity))
    answers += answer(tables, totals, tuple(range(FIRST, 9)), capacity)
    returned = [answers[HOME]] * 9
    for i in BACK_ORDER:
        returned[i] = move(answers[i], extents, -PLANE[i][0], PLANE[i][1], 0)
    patches, blocks = block_owner.shape
    rows = patches * blocks
    combined = collect(back, returned, EARLY, rows, capacity)
    late = tuple(i for i in range(9) if i not in EARLY)
    combined = collect(back, returned, late, rows, capacity, combined)
    combined = combined.reshape(patches, blocks, *combined.shape[1:])
    return owned, combined


def solution(mesh):
    return jax.shard_map(
        on_device,
        mesh=mesh,
        in_specs=(
            P(AXES, None, None),
            P(AXES, None, None),
            P(AXES, None),
            P(AXES, None),
            P(AXES, None, None),
        ),
        out_specs=(P(AXES, None, None), P(AXES, None, None, None)),
        check_vma=False,
    )
```
